512 devices in a mesh: seq: 128 (over y, x_lo, z), chan: 4 (over x_hi, core).
Axes of the slice: x: 4 (x_hi: 2, x_lo: 2; x = x_hi * 2 + x_lo), y: 8, z: 8, core: 2. Of those that a mesh axis runs over, the one named last changes fastest.
Arguments:
- gate_outer: bfloat16 [16384, 2048], P('seq', 'chan'), may hold values from -6 to 6
- gate_inner: bfloat16 [16384, 2048], P('seq', 'chan'), may hold values from -6 to 6
- signal: bfloat16 [16384, 2048], P('seq', 'chan'), may hold values from -6 to 6
- filter_raw: float32 [512, 16384], P('seq'), may hold values from -6 to 6
- cotangent: bfloat16 [16384, 2048], P('seq', 'chan'), may hold values from -6 to 6
Outputs:
- mixed_out: bfloat16 [16384, 2048], P('seq', 'chan')
- grad_outer: bfloat16 [16384, 2048], P('seq', 'chan')
- grad_inner: bfloat16 [16384, 2048], P('seq', 'chan')
- grad_signal: bfloat16 [16384, 2048], P('seq', 'chan')
- grad_filter: float32 [512, 16384], P('seq')
The draws below stay inside these ranges and needn't reach their ends.
All inputs are finite; a program needn't handle non-finite values.
Results may differ from the reference program's by a relative error of at most 0.0057.
Values may be sent and summed in bfloat16 or wider, within the bound.
No kernel may reach another device: no remote copies, remote signals or barrier semaphores. Data moves between devices by JAX's collectives and lax.ppermute only.
A program may use at most 64 MiB of HBM per device.

```python
import math
import jax
import jax.numpy as jnp

FG = 512
TOKENS = 16384
CH = 2048


def levels(rng, dims, cuts, low, top_value):
    factor_of = 1.0
    for dim, parts in cuts:
        draws = jax.random.uniform(jax.random.fold_in(jax.random.fold_in(rng, 6), dim), (parts,), jnp.float32, low / len(cuts), top_value / len(cuts))
        factor_of = factor_of * jnp.repeat(jnp.exp(draws), dims[dim] // parts).reshape((-1,) + (1,) * (len(dims) - 1 - dim))
    return factor_of


def scatter_about(stream_key, shape, width, limit, split=(), dtype=jnp.bfloat16):
    loudness = levels(stream_key, shape, split, -0.22, 0.18) if split else 1.0
    values = jax.random.normal(stream_key, shape, jnp.float32) * width * loudness
    return jnp.minimum(jnp.maximum(values, -limit), limit).astype(dtype)


def setup_inputs(seed: int = 0) -> dict:
    seeds = jax.random.split(jax.random.key(seed), 6)
    gate_outer = scatter_about(seeds[0], (TOKENS, CH), 1.0, 6.0, ((0, 128), (1, 4)))
    gate_inner = scatter_about(seeds[1], (TOKENS, CH), 1.0, 6.0, ((0, 128), (1, 4)))
    signal = scatter_about(seeds[2], (TOKENS, CH), 1.0, 6.0, ((0, 128), (1, 4)))
    filter_raw = scatter_about(seeds[3], (FG, TOKENS), 1.0, 6.0, ((0, 128),), jnp.float32)
    cotangent = scatter_about(seeds[4], (TOKENS, CH), 1.0, 6.0, ((0, 128), (1, 4)))
    return dict(gate_outer=gate_outer, gate_inner=gate_inner, signal=signal, filter_raw=filter_raw, cotangent=cotangent)


def reference(gate_outer, gate_inner, signal, filter_raw, cotangent):
    padded_len = 2 * TOKENS
    norm_scale = 1.0 / math.sqrt(TOKENS)
    filter_taps = filter_raw * norm_scale
    taps_all = jnp.tile(filter_taps, (CH // FG, 1))
    inner_prod = (gate_inner.astype(jnp.float32) * signal.astype(jnp.float32)).astype(jnp.bfloat16)
    tap_spec = jnp.fft.rfft(taps_all, n=padded_len, axis=1)
    inner_spec = jnp.fft.rfft(inner_prod.astype(jnp.float32).T, n=padded_len, axis=1)
    conv_full = jnp.fft.irfft(tap_spec * inner_spec, n=padded_len, axis=1)[:, :TOKENS]
    conv_out = conv_full.T.astype(jnp.bfloat16)
    outer_f = gate_outer.astype(jnp.float32)
    cotan_f = cotangent.astype(jnp.float32)
    conv_f = conv_out.astype(jnp.float32)
    mixed_out = (outer_f * conv_f).astype(jnp.bfloat16)
    grad_outer = (cotan_f * conv_f).astype(jnp.bfloat16)
    grad_conv = (cotan_f * outer_f).astype(jnp.bfloat16)
    grad_spec = jnp.fft.rfft(grad_conv.astype(jnp.float32).T, n=padded_len, axis=1)
    back_full = jnp.fft.irfft(jnp.conj(tap_spec) * grad_spec, n=padded_len, axis=1)[:, :TOKENS]
    grad_prod = back_full.T.astype(jnp.bfloat16)
    prod_f = grad_prod.astype(jnp.float32)
    grad_inner = (prod_f * signal.astype(jnp.float32)).astype(jnp.bfloat16)
    grad_signal = (prod_f * gate_inner.astype(jnp.float32)).astype(jnp.bfloat16)
    per_channel = jnp.fft.irfft(jnp.conj(inner_spec) * grad_spec, n=padded_len, axis=1)[:, :TOKENS]
    grad_filter = per_channel.reshape(CH // FG, FG, TOKENS).sum(axis=0) * norm_scale
    return (mixed_out, grad_outer, grad_inner, grad_signal, grad_filter)
```

```python
import math

import jax
import jax.numpy as jnp
import numpy as np
import ml_dtypes
from jax import lax
from jax.experimental import pallas as pl
from jax.experimental.pallas import tpu as pltpu
from jax.sharding import PartitionSpec as P

BF = jnp.bfloat16
F32 = jnp.float32
VMEM_BYTES = 40 * 1024 * 1024


def split_np(table):
    high = table.astype(ml_dtypes.bfloat16)
    low = (table - high.astype(np.float64)).astype(ml_dtypes.bfloat16)
    return high, low


def dft_tables(rows_n, cols_n, scale):
    length = rows_n * cols_n
    row_i = np.arange(rows_n, dtype=np.float64)
    col_i = np.arange(cols_n, dtype=np.float64)
    ang_one = -2.0 * np.pi * np.outer(row_i + 0.25, row_i) / rows_n
    ang_twid = -2.0 * np.pi * np.outer(row_i + 0.25, col_i) / length
    ang_two = 2.0 * np.pi * (np.outer(col_i, col_i) % cols_n) / cols_n
    first = np.concatenate([np.cos(ang_one), np.sin(ang_one)], axis=0)
    cos_two, sin_two = np.cos(ang_two), np.sin(ang_two)
    second = np.block([[cos_two, -sin_two], [sin_two, cos_two]])
    second_inv = second.T
    last = first.T * scale
    first_h, first_l = split_np(first)
    second_h, second_l = split_np(second)
    inv_h, inv_l = split_np(second_inv)
    last_h, last_l = split_np(last)
    return dict(
        first=np.concatenate([first_h, first_l], axis=1),
        twid=np.concatenate([np.cos(ang_twid), -np.sin(ang_twid)], axis=1).astype(np.float32),
        second=np.concatenate([second_h, second_h, second_l], axis=0),
        inverse=np.concatenate([inv_h, inv_h, inv_l], axis=0),
        last=np.concatenate([last_h, last_l, last_h], axis=1),
    )


def split_hl(value):
    high = value.astype(BF)
    low = (value - high.astype(F32)).astype(BF)
    return high, low


def dot32(left, right):
    return lax.dot_general(left, right, (((1,), (0,)), ((), ())), preferred_element_type=F32)


def pack_kernel(outer_ref, inner_ref, signal_ref, cotan_ref, out_ref, flat_ref, mix_ref):
    prod = (inner_ref[...].astype(F32) * signal_ref[...].astype(F32)).astype(BF).astype(F32)
    grad = (cotan_ref[...].astype(F32) * outer_ref[...].astype(F32)).astype(BF).astype(F32)
    count = out_ref.shape[0] // 8
    for half, value in enumerate((prod, grad)):
        flat_ref[half] = value.T
        for c in range(4):
            mix_ref[pl.ds(4 * half + c, count, stride=8), :] = flat_ref[
                half, pl.ds(c, count, stride=4), :
            ]
    out_ref[...] = mix_ref[...].astype(BF)


def second_stage(part, twid_cos, twid_sin, second):
    rows = twid_cos.shape[0]
    pieces = []
    for one in part:
        real, imag = one[:rows], one[rows:]
        turned = jnp.concatenate(
            [real * twid_cos + imag * twid_sin, imag * twid_cos - real * twid_sin], axis=1
        )
        high, low = split_hl(turned)
        pieces.append(jnp.concatenate([high, low, high], axis=1))
    return dot32(jnp.concatenate(pieces, axis=0), second)


def filter_kernel(filt_ref, first_ref, twid_ref, second_ref, out_ref, rows_ref):
    rows = twid_ref.shape[0]
    cols = twid_ref.shape[1] // 2
    for n in range(rows):
        rows_ref[pl.ds(4 * n, 4), :] = filt_ref[:, cols * n : cols * (n + 1)]
    first = first_ref[...]
    parts = []
    for f in range(4):
        high, low = split_hl(rows_ref[pl.ds(f, rows, stride=4), :])
        parts.append((high, low))
    high = jnp.concatenate([h for h, _ in parts], axis=1)
    low = jnp.concatenate([l for _, l in parts], axis=1)
    stage = dot32(first, jnp.concatenate([high, high], axis=0)) + dot32(first[:, :rows], low)
    out_ref[...] = second_stage(
        [stage[:, cols * f : cols * (f + 1)] for f in range(4)],
        twid_ref[:, :cols],
        twid_ref[:, cols:],
        second_ref[...],
    )


def conv_kernel(
    recv_ref, spec_ref, first_ref, twid_ref, second_ref, inverse_ref, last_ref,
    send_ref, corr_ref, flat_ref, back_ref, corr_mix_ref,
):
    rows = twid_ref.shape[0]
    cols = twid_ref.shape[1] // 2
    twid_cos, twid_sin = twid_ref[:, :cols], twid_ref[:, cols:]
    flat_ref[...] = recv_ref[...].astype(F32)
    columns = jnp.concatenate(
        [flat_ref[pl.ds(c, rows, stride=8), :].astype(BF) for c in range(8)], axis=1
    )
    stage = dot32(first_ref[...], jnp.concatenate([columns, columns], axis=0))
    spec = second_stage(
        [stage[:, cols * c : cols * (c + 1)] for c in range(8)],
        twid_cos, twid_sin, second_ref[...],
    )

    def parts_of(array, c):
        block = array[rows * c : rows * (c + 1)]
        return block[:, :cols], block[:, cols:]

    products = []
    for c in range(4):
        tap_r, tap_i = spec_ref[rows * c : rows * (c + 1), :cols], spec_ref[rows * c : rows * (c + 1), cols:]
        in_r, in_i = parts_of(spec, c)
        gr_r, gr_i = parts_of(spec, 4 + c)
        products.append((4 * 0 + c, tap_r * in_r - tap_i * in_i, tap_r * in_i + tap_i * in_r))
        products.append((4 * 1 + c, tap_r * gr_r + tap_i * gr_i, tap_r * gr_i - tap_i * gr_r))
        products.append((4 * 2 + c, in_r * gr_r + in_i * gr_i, in_r * gr_i - in_i * gr_r))
    products.sort(key=lambda item: item[0])
    pieces = []
    for _, real, imag in products:
        high, low = split_hl(jnp.concatenate([real, imag], axis=1))
        pieces.append(jnp.concatenate([high, low, high], axis=1))
    turned = dot32(jnp.concatenate(pieces, axis=0), inverse_ref[...])
    columns = []
    for c in range(12):
        real, imag = parts_of(turned, c)
        value = jnp.concatenate(
            [real * twid_cos - imag * twid_sin, imag * twid_cos + real * twid_sin], axis=0
        )
        high, low = split_hl(value)
        columns.append(jnp.concatenate([high, high, low], axis=0))
    result = dot32(last_ref[...], jnp.concatenate(columns, axis=1))
    for c in range(8):
        back_ref[pl.ds(c, rows, stride=8), :] = result[:, cols * c : cols * (c + 1)]
    send_ref[...] = back_ref[...].astype(BF)
    for c in range(4):
        corr_mix_ref[pl.ds(c, rows, stride=4), :] = result[:, cols * (8 + c) : cols * (9 + c)]
    corr_ref[...] = corr_mix_ref[...].astype(corr_ref.dtype)


def gate_kernel(
    recv_ref, outer_ref, inner_ref, signal_ref, cotan_ref,
    mixed_ref, gouter_ref, ginner_ref, gsignal_ref, flat_ref, mix_ref,
):
    count = recv_ref.shape[0] // 8
    flat_ref[...] = recv_ref[...].astype(F32)
    for c in range(8):
        mix_ref[c // 4, pl.ds(c % 4, count, stride=4), :] = flat_ref[pl.ds(c, count, stride=8), :]
    conv = mix_ref[0].T
    prod = mix_ref[1].T
    mixed_ref[...] = (outer_ref[...].astype(F32) * conv).astype(BF)
    gouter_ref[...] = (cotan_ref[...].astype(F32) * conv).astype(BF)
    ginner_ref[...] = (prod * signal_ref[...].astype(F32)).astype(BF)
    gsignal_ref[...] = (prod * inner_ref[...].astype(F32)).astype(BF)


def sum_kernel(part_ref, out_ref):
    rows = part_ref.shape[1] // 4
    total = part_ref[0].astype(F32)
    for g in range(1, part_ref.shape[0]):
        total = total + part_ref[g].astype(F32)
    for n in range(rows):
        out_ref[:, 128 * n : 128 * (n + 1)] = total[4 * n : 4 * n + 4, :]


def call(kernel, out_shape, scratch, flops=0, nbytes=0):
    return pl.pallas_call(
        kernel,
        out_shape=out_shape,
        scratch_shapes=scratch,
        compiler_params=pltpu.CompilerParams(vmem_limit_bytes=VMEM_BYTES),
        cost_estimate=pl.CostEstimate(flops=flops, bytes_accessed=nbytes, transcendentals=0),
    )


def body(gate_outer, gate_inner, signal, filter_raw, cotangent):
    tok_rows, chan_cols = gate_outer.shape
    seq_parts = lax.axis_size("seq")
    rows, cols = seq_parts, tok_rows
    seq_len = rows * cols
    tables = dft_tables(rows, cols, 1.0 / math.sqrt(seq_len) / seq_len)
    first, twid = jnp.asarray(tables["first"]), jnp.asarray(tables["twid"])
    second, inverse = jnp.asarray(tables["second"]), jnp.asarray(tables["inverse"])
    last = jnp.asarray(tables["last"])
    wide = 8 * rows
    packed = call(
        pack_kernel,
        jax.ShapeDtypeStruct((wide, cols), BF),
        [pltpu.VMEM((2, chan_cols, tok_rows), F32), pltpu.VMEM((wide, cols), F32)],
        nbytes=6 * 2 * tok_rows * chan_cols,
    )(gate_outer, gate_inner, signal, cotangent)
    received = lax.all_to_all(packed.reshape(rows, 8, cols), "seq", 0, 0, tiled=True)
    tap_spec = call(
        filter_kernel,
        jax.ShapeDtypeStruct((4 * rows, 2 * cols), F32),
        [pltpu.VMEM((4 * rows, cols), F32)],
        flops=10**9, nbytes=10**6,
    )(filter_raw, first, twid, second)
    send, corr = call(
        conv_kernel,
        (
            jax.ShapeDtypeStruct((wide, cols), BF),
            jax.ShapeDtypeStruct((4 * rows, cols), BF),
        ),
        [
            pltpu.VMEM((wide, cols), F32),
            pltpu.VMEM((wide, cols), F32),
            pltpu.VMEM((4 * rows, cols), F32),
        ],
        flops=3 * 10**9, nbytes=2 * 10**6,
    )(received.reshape(wide, cols), tap_spec, first, twid, second, inverse, last)
    parts = lax.all_gather(corr, "chan", axis=0, tiled=False)
    returned = lax.all_to_all(send.reshape(rows, 8, cols), "seq", 0, 0, tiled=True)
    grad_filter = call(
        sum_kernel,
        jax.ShapeDtypeStruct(filter_raw.shape, F32),
        [],
        nbytes=10**6,
    )(parts)
    outs = call(
        gate_kernel,
        tuple(jax.ShapeDtypeStruct((tok_rows, chan_cols), BF) for _ in range(4)),
        [pltpu.VMEM((wide, cols), F32), pltpu.VMEM((2, chan_cols, tok_rows), F32)],
        nbytes=10 * 2 * tok_rows * chan_cols,
    )(returned.reshape(wide, cols), gate_outer, gate_inner, signal, cotangent)
    return (*outs, grad_filter)


def solution(mesh):
    in_specs = (
        P("seq", "chan"),
        P("seq", "chan"),
        P("seq", "chan"),
        P("seq", None),
        P("seq", "chan"),
    )
    out_specs = (
        P("seq", "chan"),
        P("seq", "chan"),
        P("seq", "chan"),
        P("seq", "chan"),
        P("seq", None),
    )
    return jax.shard_map(body, mesh=mesh, in_specs=in_specs, out_specs=out_specs, check_vma=False)
```

```python
import functools
import math

import jax
import jax.numpy as jnp
import numpy as np
import ml_dtypes
from jax import lax
from jax.experimental import pallas as pl
from jax.experimental.pallas import tpu as pltpu
from jax.sharding import PartitionSpec as P

BF = jnp.bfloat16
F32 = jnp.float32
VMEM_BYTES = 40 * 1024 * 1024
VMEM_MOST = 60 * 1024 * 1024


def member_order(count):
    flip = count // 2
    return [r ^ flip for r in range(count)], flip


def flipped_copy(store, load, count, flip, height):
    run = flip & -flip if flip else count
    for start in range(0, count, run):
        source = start ^ flip
        store(slice(start * height, (start + run) * height), load(slice(source * height, (source + run) * height)))


def split_np(table):
    high = table.astype(ml_dtypes.bfloat16)
    low = (table - high.astype(np.float64)).astype(ml_dtypes.bfloat16)
    return high, low


def dft_tables(rows_n, cols_n, scale, order):
    length = rows_n * cols_n
    row_i = np.arange(rows_n, dtype=np.float64)
    col_i = np.arange(cols_n, dtype=np.float64)
    ang_one = -2.0 * np.pi * np.outer(row_i + 0.25, row_i[order]) / rows_n
    ang_twid = -2.0 * np.pi * np.outer(row_i + 0.25, col_i) / length
    ang_two = 2.0 * np.pi * (np.outer(col_i, col_i) % cols_n) / cols_n
    first = np.concatenate([np.cos(ang_one), np.sin(ang_one)], axis=0)
    cos_two, sin_two = np.cos(ang_two), np.sin(ang_two)
    second = np.block([[cos_two, -sin_two], [sin_two, cos_two]])
    second_inv = second.T
    last = first.T * scale
    first_h, first_l = split_np(first)
    second_h, second_l = split_np(second)
    inv_h, inv_l = split_np(second_inv)
    last_h, last_l = split_np(last)
    return dict(
        first=np.concatenate([first_h, first_l], axis=1),
        twid=np.concatenate([np.cos(ang_twid), -np.sin(ang_twid)], axis=1).astype(np.float32),
        second=np.concatenate([second_h, second_h, second_l], axis=0),
        inverse=np.concatenate([inv_h, inv_h, inv_l], axis=0),
        last=np.concatenate([last_h, last_l, last_h], axis=1),
    )


def split_hl(value):
    high = value.astype(BF)
    low = (value - high.astype(F32)).astype(BF)
    return high, low


def dot32(left, right):
    return lax.dot_general(left, right, (((1,), (0,)), ((), ())), preferred_element_type=F32)


def pack_kernel(
    flip, outer_ref, inner_ref, signal_ref, cotan_ref, out_ref, held_ref, flat_ref, mix_ref, sems
):
    count = out_ref.shape[0] // 8
    sources = (inner_ref, signal_ref, cotan_ref, outer_ref)
    copies = [
        pltpu.make_async_copy(ref, held_ref.at[k], sems.at[k]) for k, ref in enumerate(sources)
    ]
    for copy in copies:
        copy.start()
    for half in range(2):
        copies[2 * half].wait()
        copies[2 * half + 1].wait()
        left, right = held_ref[2 * half].astype(F32), held_ref[2 * half + 1].astype(F32)
        flat_ref[half] = (left * right).astype(BF).astype(F32).T
        for c in range(4):
            mix_ref[pl.ds(4 * half + c, count, stride=8), :] = flat_ref[
                half, pl.ds(c, count, stride=4), :
            ]

    def store(rows, value):
        out_ref[rows, :] = value

    flipped_copy(store, lambda rows: mix_ref[rows, :].astype(BF), count, flip, 8)


def second_stage(part, twid_cos, twid_sin, second):
    rows = twid_cos.shape[0]
    pieces = []
    for one in part:
        real, imag = one[:rows], one[rows:]
        turned = jnp.concatenate(
            [real * twid_cos + imag * twid_sin, imag * twid_cos - real * twid_sin], axis=1
        )
        high, low = split_hl(turned)
        pieces.append(jnp.concatenate([high, low, high], axis=1))
    return dot32(jnp.concatenate(pieces, axis=0), second)


def filter_kernel(flip, filt_ref, first_ref, twid_ref, second_ref, out_ref, rows_ref):
    rows = twid_ref.shape[0]
    cols = twid_ref.shape[1] // 2
    for n in range(rows):
        rows_ref[pl.ds(4 * (n ^ flip), 4), :] = filt_ref[:, cols * n : cols * (n + 1)]
    first = first_ref[...]
    parts = []
    for f in range(4):
        high, low = split_hl(rows_ref[pl.ds(f, rows, stride=4), :])
        parts.append((high, low))
    high = jnp.concatenate([h for h, _ in parts], axis=1)
    low = jnp.concatenate([l for _, l in parts], axis=1)
    stage = dot32(first, jnp.concatenate([high, high], axis=0)) + dot32(first[:, :rows], low)
    out_ref[...] = second_stage(
        [stage[:, cols * f : cols * (f + 1)] for f in range(4)],
        twid_ref[:, :cols],
        twid_ref[:, cols:],
        second_ref[...],
    )


def conv_kernel(
    recv_ref, spec_ref, first_ref, twid_ref, second_ref, inverse_ref, last_ref,
    send_ref, corr_ref, flat_ref, back_ref, corr_mix_ref,
):
    rows = twid_ref.shape[0]
    cols = twid_ref.shape[1] // 2
    twid_cos, twid_sin = twid_ref[:, :cols], twid_ref[:, cols:]
    flat_ref[...] = recv_ref[...].astype(F32)
    columns = jnp.concatenate(
        [flat_ref[pl.ds(c, rows, stride=8), :].astype(BF) for c in range(8)], axis=1
    )
    stage = dot32(first_ref[...], jnp.concatenate([columns, columns], axis=0))
    spec = second_stage(
        [stage[:, cols * c : cols * (c + 1)] for c in range(8)],
        twid_cos, twid_sin, second_ref[...],
    )

    def parts_of(array, c):
        block = array[rows * c : rows * (c + 1)]
        return block[:, :cols], block[:, cols:]

    products = []
    for c in range(4):
        tap_r, tap_i = spec_ref[rows * c : rows * (c + 1), :cols], spec_ref[rows * c : rows * (c + 1), cols:]
        in_r, in_i = parts_of(spec, c)
        gr_r, gr_i = parts_of(spec, 4 + c)
        products.append((4 * 0 + c, tap_r * in_r - tap_i * in_i, tap_r * in_i + tap_i * in_r))
        products.append((4 * 1 + c, tap_r * gr_r + tap_i * gr_i, tap_r * gr_i - tap_i * gr_r))
        products.append((4 * 2 + c, in_r * gr_r + in_i * gr_i, in_r * gr_i - in_i * gr_r))
    products.sort(key=lambda item: item[0])
    pieces = []
    for _, real, imag in products:
        high, low = split_hl(jnp.concatenate([real, imag], axis=1))
        pieces.append(jnp.concatenate([high, low, high], axis=1))
    turned = dot32(jnp.concatenate(pieces, axis=0), inverse_ref[...])
    columns = []
    for c in range(12):
        real, imag = parts_of(turned, c)
        value = jnp.concatenate(
            [real * twid_cos - imag * twid_sin, imag * twid_cos + real * twid_sin], axis=0
        )
        high, low = split_hl(value)
        columns.append(jnp.concatenate([high, high, low], axis=0))
    result = dot32(last_ref[...], jnp.concatenate(columns, axis=1))
    for c in range(8):
        back_ref[pl.ds(c, rows, stride=8), :] = result[:, cols * c : cols * (c + 1)]
    send_ref[...] = back_ref[...].astype(BF)
    for c in range(4):
        corr_mix_ref[pl.ds(c, rows, stride=4), :] = result[:, cols * (8 + c) : cols * (9 + c)]
    corr_ref[...] = corr_mix_ref[...].astype(corr_ref.dtype)


def gate_kernel(
    flip, recv_ref, outer_ref, inner_ref, signal_ref, cotan_ref, part_ref,
    mixed_ref, gouter_ref, ginner_ref, gsignal_ref, gfilter_ref, flat_ref, mix_ref,
):
    total = part_ref[0].astype(F32)
    for g in range(1, part_ref.shape[0]):
        total = total + part_ref[g].astype(F32)
    count = recv_ref.shape[0] // 8
    cols = recv_ref.shape[1]
    for n in range(count):
        gfilter_ref[:, cols * (n ^ flip) : cols * ((n ^ flip) + 1)] = total[4 * n : 4 * n + 4, :]

    def store(rows, value):
        flat_ref[rows, :] = value

    flipped_copy(store, lambda rows: recv_ref[rows, :].astype(F32), count, flip, 8)
    for c in range(8):
        mix_ref[c // 4, pl.ds(c % 4, count, stride=4), :] = flat_ref[pl.ds(c, count, stride=8), :]
    conv = mix_ref[0].T
    prod = mix_ref[1].T
    mixed_ref[...] = (outer_ref[...].astype(F32) * conv).astype(BF)
    gouter_ref[...] = (cotan_ref[...].astype(F32) * conv).astype(BF)
    ginner_ref[...] = (prod * signal_ref[...].astype(F32)).astype(BF)
    gsignal_ref[...] = (prod * inner_ref[...].astype(F32)).astype(BF)


def call(kernel, out_shape, scratch, flops=0, nbytes=0, vmem=VMEM_BYTES, **specs):
    return pl.pallas_call(
        kernel,
        out_shape=out_shape,
        scratch_shapes=scratch,
        compiler_params=pltpu.CompilerParams(vmem_limit_bytes=vmem),
        **specs,
        cost_estimate=pl.CostEstimate(flops=flops, bytes_accessed=nbytes, transcendentals=0),
    )


def exchange(chunks, order):
    return lax.all_to_all(chunks, "seq", 0, 0, axis_index_groups=[order], tiled=True)


def body(gate_outer, gate_inner, signal, filter_raw, cotangent):
    tok_rows, chan_cols = gate_outer.shape
    seq_parts = lax.axis_size("seq")
    rows, cols = seq_parts, tok_rows
    seq_len = rows * cols
    order, flip = member_order(seq_parts)
    tables = dft_tables(rows, cols, 1.0 / math.sqrt(seq_len) / seq_len, order)
    first, twid = jnp.asarray(tables["first"]), jnp.asarray(tables["twid"])
    second, inverse = jnp.asarray(tables["second"]), jnp.asarray(tables["inverse"])
    last = jnp.asarray(tables["last"])
    wide = 8 * rows
    packed = call(
        functools.partial(pack_kernel, flip),
        jax.ShapeDtypeStruct((wide, cols), BF),
        [
            pltpu.VMEM((4, tok_rows, chan_cols), BF),
            pltpu.VMEM((2, chan_cols, tok_rows), F32),
            pltpu.VMEM((wide, cols), F32),
            pltpu.SemaphoreType.DMA((4,)),
        ],
        nbytes=6 * 2 * tok_rows * chan_cols,
        vmem=VMEM_MOST,
        in_specs=[pl.BlockSpec(memory_space=pltpu.HBM)] * 4,
    )(gate_outer, gate_inner, signal, cotangent)
    received = exchange(packed.reshape(rows, 8, cols), order)
    tap_spec = call(
        functools.partial(filter_kernel, flip),
        jax.ShapeDtypeStruct((4 * rows, 2 * cols), F32),
        [pltpu.VMEM((4 * rows, cols), F32)],
        flops=10**9, nbytes=10**6,
    )(filter_raw, first, twid, second)
    send, corr = call(
        conv_kernel,
        (
            jax.ShapeDtypeStruct((wide, cols), BF),
            jax.ShapeDtypeStruct((4 * rows, cols), BF),
        ),
        [
            pltpu.VMEM((wide, cols), F32),
            pltpu.VMEM((wide, cols), F32),
            pltpu.VMEM((4 * rows, cols), F32),
        ],
        flops=3 * 10**9, nbytes=2 * 10**6,
    )(received.reshape(wide, cols), tap_spec, first, twid, second, inverse, last)
    parts = lax.all_gather(corr, "chan", axis=0, tiled=False)
    returned = exchange(send.reshape(rows, 8, cols), order)
    block = jax.ShapeDtypeStruct((tok_rows, chan_cols), BF)
    return call(
        functools.partial(gate_kernel, flip),
        (block, block, block, block, jax.ShapeDtypeStruct(filter_raw.shape, F32)),
        [pltpu.VMEM((wide, cols), F32), pltpu.VMEM((2, chan_cols, tok_rows), F32)],
        nbytes=12 * 2 * tok_rows * chan_cols,
    )(returned.reshape(wide, cols), gate_outer, gate_inner, signal, cotangent, parts)


def solution(mesh):
    in_specs = (
        P("seq", "chan"),
        P("seq", "chan"),
        P("seq", "chan"),
        P("seq", None),
        P("seq", "chan"),
    )
    out_specs = (
        P("seq", "chan"),
        P("seq", "chan"),
        P("seq", "chan"),
        P("seq", "chan"),
        P("seq", None),
    )
    return jax.shard_map(body, mesh=mesh, in_specs=in_specs, out_specs=out_specs, check_vma=False)
```

```python
import functools
import math

import jax
import jax.numpy as jnp
import numpy as np
import ml_dtypes
from jax import lax
from jax.experimental import pallas as pl
from jax.experimental.pallas import tpu as pltpu
from jax.sharding import PartitionSpec as P

BF = jnp.bfloat16
F32 = jnp.float32
VMEM_BYTES = 40 * 1024 * 1024
VMEM_MOST = 60 * 1024 * 1024


def member_order(count):
    flip = count // 2 + count // 4
    return [r ^ flip for r in range(count)], flip


def flipped_copy(store, load, count, flip, height):
    run = flip & -flip if flip else count
    for start in range(0, count, run):
        source = start ^ flip
        store(slice(start * height, (start + run) * height), load(slice(source * height, (source + run) * height)))


def split_np(table):
    high = table.astype(ml_dtypes.bfloat16)
    low = (table - high.astype(np.float64)).astype(ml_dtypes.bfloat16)
    return high, low


def dft_tables(rows_n, cols_n, scale, order):
    length = rows_n * cols_n
    row_i = np.arange(rows_n, dtype=np.float64)
    col_i = np.arange(cols_n, dtype=np.float64)
    ang_one = -2.0 * np.pi * np.outer(row_i + 0.25, row_i[order]) / rows_n
    ang_twid = -2.0 * np.pi * np.outer(row_i + 0.25, col_i) / length
    ang_two = 2.0 * np.pi * (np.outer(col_i, col_i) % cols_n) / cols_n
    first = np.concatenate([np.cos(ang_one), np.sin(ang_one)], axis=0)
    cos_two, sin_two = np.cos(ang_two), np.sin(ang_two)
    second = np.block([[cos_two, -sin_two], [sin_two, cos_two]])
    second_inv = second.T
    last = first.T * scale
    first_h, first_l = split_np(first)
    second_h, second_l = split_np(second)
    inv_h, inv_l = split_np(second_inv)
    last_h, last_l = split_np(last)
    return dict(
        first=np.concatenate([first_h, first_l], axis=1),
        twid=np.concatenate([np.cos(ang_twid), -np.sin(ang_twid)], axis=1).astype(np.float32),
        second=np.concatenate([second_h, second_h, second_l], axis=0),
        inverse=np.concatenate([inv_h, inv_l], axis=0),
        last=np.concatenate([last_h, last_l], axis=1),
    )


def split_hl(value):
    high = value.astype(BF)
    low = (value - high.astype(F32)).astype(BF)
    return high, low


def dot32(left, right):
    return lax.dot_general(left, right, (((1,), (0,)), ((), ())), preferred_element_type=F32)


def pack_kernel(
    flip, outer_ref, inner_ref, signal_ref, cotan_ref, out_ref, held_ref, flat_ref, mix_ref, sems
):
    count = out_ref.shape[0] // 8
    sources = (inner_ref, signal_ref, cotan_ref, outer_ref)
    copies = [
        pltpu.make_async_copy(ref, held_ref.at[k], sems.at[k]) for k, ref in enumerate(sources)
    ]
    for copy in copies:
        copy.start()
    for half in range(2):
        copies[2 * half].wait()
        copies[2 * half + 1].wait()
        left, right = held_ref[2 * half].astype(F32), held_ref[2 * half + 1].astype(F32)
        flat_ref[half] = (left * right).astype(BF).astype(F32).T
        for c in range(4):
            mix_ref[pl.ds(4 * half + c, count, stride=8), :] = flat_ref[
                half, pl.ds(c, count, stride=4), :
            ]

    def store(rows, value):
        out_ref[rows, :] = value

    flipped_copy(store, lambda rows: mix_ref[rows, :].astype(BF), count, flip, 8)


def second_stage(part, twid_cos, twid_sin, second):
    rows = twid_cos.shape[0]
    pieces = []
    for one in part:
        real, imag = one[:rows], one[rows:]
        turned = jnp.concatenate(
            [real * twid_cos + imag * twid_sin, imag * twid_cos - real * twid_sin], axis=1
        )
        high, low = split_hl(turned)
        pieces.append(jnp.concatenate([high, low, high], axis=1))
    return dot32(jnp.concatenate(pieces, axis=0), second)


def filter_kernel(flip, filt_ref, first_ref, twid_ref, second_ref, out_ref, rows_ref):
    rows = twid_ref.shape[0]
    cols = twid_ref.shape[1] // 2
    for n in range(rows):
        rows_ref[pl.ds(4 * (n ^ flip), 4), :] = filt_ref[:, cols * n : cols * (n + 1)]
    first = first_ref[...]
    parts = []
    for f in range(4):
        high, low = split_hl(rows_ref[pl.ds(f, rows, stride=4), :])
        parts.append((high, low))
    high = jnp.concatenate([h for h, _ in parts], axis=1)
    low = jnp.concatenate([l for _, l in parts], axis=1)
    stage = dot32(first, jnp.concatenate([high, high], axis=0)) + dot32(first[:, :rows], low)
    out_ref[...] = second_stage(
        [stage[:, cols * f : cols * (f + 1)] for f in range(4)],
        twid_ref[:, :cols],
        twid_ref[:, cols:],
        second_ref[...],
    )


def conv_kernel(
    recv_ref, spec_ref, first_ref, twid_ref, second_ref, inverse_ref, last_ref,
    send_ref, corr_ref, flat_ref, back_ref, corr_mix_ref,
):
    rows = twid_ref.shape[0]
    cols = twid_ref.shape[1] // 2
    twid_cos, twid_sin = twid_ref[:, :cols], twid_ref[:, cols:]
    flat_ref[...] = recv_ref[...].astype(F32)
    columns = jnp.concatenate(
        [flat_ref[pl.ds(c, rows, stride=8), :].astype(BF) for c in range(8)], axis=1
    )
    stage = dot32(first_ref[...], jnp.concatenate([columns, columns], axis=0))
    spec = second_stage(
        [stage[:, cols * c : cols * (c + 1)] for c in range(8)],
        twid_cos, twid_sin, second_ref[...],
    )

    def parts_of(array, c):
        block = array[rows * c : rows * (c + 1)]
        return block[:, :cols], block[:, cols:]

    products = []
    for c in range(4):
        tap_r, tap_i = spec_ref[rows * c : rows * (c + 1), :cols], spec_ref[rows * c : rows * (c + 1), cols:]
        in_r, in_i = parts_of(spec, c)
        gr_r, gr_i = parts_of(spec, 4 + c)
        products.append((4 * 0 + c, tap_r * in_r - tap_i * in_i, tap_r * in_i + tap_i * in_r))
        products.append((4 * 1 + c, tap_r * gr_r + tap_i * gr_i, tap_r * gr_i - tap_i * gr_r))
        products.append((4 * 2 + c, in_r * gr_r + in_i * gr_i, in_r * gr_i - in_i * gr_r))
    products.sort(key=lambda item: item[0])
    pieces = []
    for _, real, imag in products:
        value = jnp.concatenate([real, imag], axis=1).astype(BF)
        pieces.append(jnp.concatenate([value, value], axis=1))
    turned = dot32(jnp.concatenate(pieces, axis=0), inverse_ref[...])
    columns = []
    for c in range(12):
        real, imag = parts_of(turned, c)
        value = jnp.concatenate(
            [real * twid_cos - imag * twid_sin, imag * twid_cos + real * twid_sin], axis=0
        ).astype(BF)
        columns.append(jnp.concatenate([value, value], axis=0))
    result = dot32(last_ref[...], jnp.concatenate(columns, axis=1))
    for c in range(8):
        back_ref[pl.ds(c, rows, stride=8), :] = result[:, cols * c : cols * (c + 1)]
    send_ref[...] = back_ref[...].astype(BF)
    for c in range(4):
        corr_mix_ref[pl.ds(c, rows, stride=4), :] = result[:, cols * (8 + c) : cols * (9 + c)]
    corr_ref[...] = corr_mix_ref[...].astype(corr_ref.dtype)


def gate_kernel(
    flip, recv_ref, outer_ref, inner_ref, signal_ref, cotan_ref, part_ref,
    mixed_ref, gouter_ref, ginner_ref, gsignal_ref, gfilter_ref, flat_ref, mix_ref,
):
    total = part_ref[0].astype(F32)
    for g in range(1, part_ref.shape[0]):
        total = total + part_ref[g].astype(F32)
    count = recv_ref.shape[0] // 8
    cols = recv_ref.shape[1]
    for n in range(count):
        gfilter_ref[:, cols * (n ^ flip) : cols * ((n ^ flip) + 1)] = total[4 * n : 4 * n + 4, :]

    def store(rows, value):
        flat_ref[rows, :] = value

    flipped_copy(store, lambda rows: recv_ref[rows, :].astype(F32), count, flip, 8)
    for c in range(8):
        mix_ref[c // 4, pl.ds(c % 4, count, stride=4), :] = flat_ref[pl.ds(c, count, stride=8), :]
    conv = mix_ref[0].T
    prod = mix_ref[1].T
    mixed_ref[...] = (outer_ref[...].astype(F32) * conv).astype(BF)
    gouter_ref[...] = (cotan_ref[...].astype(F32) * conv).astype(BF)
    ginner_ref[...] = (prod * signal_ref[...].astype(F32)).astype(BF)
    gsignal_ref[...] = (prod * inner_ref[...].astype(F32)).astype(BF)


def call(kernel, out_shape, scratch, flops=0, nbytes=0, vmem=VMEM_BYTES, **specs):
    return pl.pallas_call(
        kernel,
        out_shape=out_shape,
        scratch_shapes=scratch,
        compiler_params=pltpu.CompilerParams(vmem_limit_bytes=vmem),
        **specs,
        cost_estimate=pl.CostEstimate(flops=flops, bytes_accessed=nbytes, transcendentals=0),
    )


def exchange(chunks, order):
    return lax.all_to_all(chunks, "seq", 0, 0, axis_index_groups=[order], tiled=True)


def body(gate_outer, gate_inner, signal, filter_raw, cotangent):
    tok_rows, chan_cols = gate_outer.shape
    seq_parts = lax.axis_size("seq")
    rows, cols = seq_parts, tok_rows
    seq_len = rows * cols
    order, flip = member_order(seq_parts)
    tables = dft_tables(rows, cols, 1.0 / math.sqrt(seq_len) / seq_len, order)
    first, twid = jnp.asarray(tables["first"]), jnp.asarray(tables["twid"])
    second, inverse = jnp.asarray(tables["second"]), jnp.asarray(tables["inverse"])
    last = jnp.asarray(tables["last"])
    wide = 8 * rows
    packed = call(
        functools.partial(pack_kernel, flip),
        jax.ShapeDtypeStruct((wide, cols), BF),
        [
            pltpu.VMEM((4, tok_rows, chan_cols), BF),
            pltpu.VMEM((2, chan_cols, tok_rows), F32),
            pltpu.VMEM((wide, cols), F32),
            pltpu.SemaphoreType.DMA((4,)),
        ],
        nbytes=6 * 2 * tok_rows * chan_cols,
        vmem=VMEM_MOST,
        in_specs=[pl.BlockSpec(memory_space=pltpu.HBM)] * 4,
    )(gate_outer, gate_inner, signal, cotangent)
    received = exchange(packed.reshape(rows, 8, cols), order)
    tap_spec = call(
        functools.partial(filter_kernel, flip),
        jax.ShapeDtypeStruct((4 * rows, 2 * cols), F32),
        [pltpu.VMEM((4 * rows, cols), F32)],
        flops=10**9, nbytes=10**6,
    )(filter_raw, first, twid, second)
    send, corr = call(
        conv_kernel,
        (
            jax.ShapeDtypeStruct((wide, cols), BF),
            jax.ShapeDtypeStruct((4 * rows, cols), BF),
        ),
        [
            pltpu.VMEM((wide, cols), F32),
            pltpu.VMEM((wide, cols), F32),
            pltpu.VMEM((4 * rows, cols), F32),
        ],
        flops=3 * 10**9, nbytes=2 * 10**6,
    )(received.reshape(wide, cols), tap_spec, first, twid, second, inverse, last)
    parts = lax.all_gather(corr, "chan", axis=0, tiled=False)
    returned = exchange(send.reshape(rows, 8, cols), order)
    block = jax.ShapeDtypeStruct((tok_rows, chan_cols), BF)
    return call(
        functools.partial(gate_kernel, flip),
        (block, block, block, block, jax.ShapeDtypeStruct(filter_raw.shape, F32)),
        [pltpu.VMEM((wide, cols), F32), pltpu.VMEM((2, chan_cols, tok_rows), F32)],
        nbytes=12 * 2 * tok_rows * chan_cols,
    )(returned.reshape(wide, cols), gate_outer, gate_inner, signal, cotangent, parts)


def solution(mesh):
    in_specs = (
        P("seq", "chan"),
        P("seq", "chan"),
        P("seq", "chan"),
        P("seq", None),
        P("seq", "chan"),
    )
    out_specs = (
        P("seq", "chan"),
        P("seq", "chan"),
        P("seq", "chan"),
        P("seq", "chan"),
        P("seq", None),
    )
    return jax.shard_map(body, mesh=mesh, in_specs=in_specs, out_specs=out_specs, check_vma=False)
```

```python
import functools
import math

import jax
import jax.numpy as jnp
import numpy as np
import ml_dtypes
from jax import lax
from jax.experimental import pallas as pl
from jax.experimental.pallas import tpu as pltpu
from jax.sharding import PartitionSpec as P

BF = jnp.bfloat16
F32 = jnp.float32
VMEM_BYTES = 40 * 1024 * 1024
VMEM_MOST = 60 * 1024 * 1024


def member_order(count):
    flip = count // 2 + count // 4
    return [r ^ flip for r in range(count)], flip


def flipped_copy(store, load, count, flip, height):
    run = flip & -flip if flip else count
    for start in range(0, count, run):
        source = start ^ flip
        store(slice(start * height, (start + run) * height), load(slice(source * height, (source + run) * height)))


def split_np(table):
    high = table.astype(ml_dtypes.bfloat16)
    low = (table - high.astype(np.float64)).astype(ml_dtypes.bfloat16)
    return high, low


def dft_tables(rows_n, cols_n, scale, order):
    length = rows_n * cols_n
    row_i = np.arange(rows_n, dtype=np.float64)
    col_i = np.arange(cols_n, dtype=np.float64)
    ang_one = -2.0 * np.pi * np.outer(row_i + 0.25, row_i[order]) / rows_n
    ang_twid = -2.0 * np.pi * np.outer(row_i + 0.25, col_i) / length
    ang_two = 2.0 * np.pi * (np.outer(col_i, col_i) % cols_n) / cols_n
    first = np.concatenate([np.cos(ang_one), np.sin(ang_one)], axis=0)
    cos_two, sin_two = np.cos(ang_two), np.sin(ang_two)
    second = np.block([[cos_two, -sin_two], [sin_two, cos_two]])
    second_inv = second.T
    last = first.T * scale
    first_h, first_l = split_np(first)
    second_h, second_l = split_np(second)
    inv_h, inv_l = split_np(second_inv)
    last_h, last_l = split_np(last)
    return dict(
        first=np.concatenate([first_h, first_l], axis=1),
        twid=np.concatenate([np.cos(ang_twid), -np.sin(ang_twid)], axis=1).astype(np.float32),
        second=np.concatenate([second_h, second_h, second_l], axis=0),
        inverse=np.concatenate([inv_h, inv_l], axis=0),
        last=np.concatenate([last_h, last_l], axis=1),
    )


def split_hl(value):
    high = value.astype(BF)
    low = (value - high.astype(F32)).astype(BF)
    return high, low


def dot32(left, right):
    return lax.dot_general(left, right, (((1,), (0,)), ((), ())), preferred_element_type=F32)


def pack_kernel(
    flip, outer_ref, inner_ref, signal_ref, cotan_ref, out_ref, held_ref, flat_ref, mix_ref, sems
):
    count = out_ref.shape[0] // 8
    sources = (inner_ref, signal_ref, cotan_ref, outer_ref)
    copies = [
        pltpu.make_async_copy(ref, held_ref.at[k], sems.at[k]) for k, ref in enumerate(sources)
    ]
    for copy in copies:
        copy.start()
    for half in range(2):
        copies[2 * half].wait()
        copies[2 * half + 1].wait()
        left, right = held_ref[2 * half].astype(F32), held_ref[2 * half + 1].astype(F32)
        flat_ref[half] = (left * right).astype(BF).astype(F32).T
        for c in range(4):
            mix_ref[pl.ds(4 * half + c, count, stride=8), :] = flat_ref[
                half, pl.ds(c, count, stride=4), :
            ]

    def store(rows, value):
        out_ref[rows, :] = value

    flipped_copy(store, lambda rows: mix_ref[rows, :].astype(BF), count, flip, 8)


def second_stage(part, twid_cos, twid_sin, second):
    rows = twid_cos.shape[0]
    pieces = []
    for one in part:
        real, imag = one[:rows], one[rows:]
        turned = jnp.concatenate(
            [real * twid_cos + imag * twid_sin, imag * twid_cos - real * twid_sin], axis=1
        )
        high, low = split_hl(turned)
        pieces.append(jnp.concatenate([high, low, high], axis=1))
    return dot32(jnp.concatenate(pieces, axis=0), second)


def filter_kernel(flip, filt_ref, first_ref, twid_ref, second_ref, out_ref, rows_ref):
    rows = twid_ref.shape[0]
    cols = twid_ref.shape[1] // 2
    for n in range(rows):
        rows_ref[pl.ds(4 * (n ^ flip), 4), :] = filt_ref[:, cols * n : cols * (n + 1)]
    first = first_ref[...]
    parts = []
    for f in range(4):
        high, low = split_hl(rows_ref[pl.ds(f, rows, stride=4), :])
        parts.append((high, low))
    high = jnp.concatenate([h for h, _ in parts], axis=1)
    low = jnp.concatenate([l for _, l in parts], axis=1)
    stage = dot32(first, jnp.concatenate([high, high], axis=0)) + dot32(first[:, :rows], low)
    out_ref[...] = second_stage(
        [stage[:, cols * f : cols * (f + 1)] for f in range(4)],
        twid_ref[:, :cols],
        twid_ref[:, cols:],
        second_ref[...],
    )


def conv_kernel(
    recv_ref, spec_ref, first_ref, twid_ref, second_ref, inverse_ref, last_ref,
    send_ref, corr_ref, flat_ref, back_ref, corr_mix_ref, done_ref, sem,
):
    rows = twid_ref.shape[0]
    cols = twid_ref.shape[1] // 2
    twid_cos, twid_sin = twid_ref[:, :cols], twid_ref[:, cols:]
    flat_ref[...] = recv_ref[...].astype(F32)
    columns = jnp.concatenate(
        [flat_ref[pl.ds(c, rows, stride=8), :].astype(BF) for c in range(8)], axis=1
    )
    stage = dot32(first_ref[...], jnp.concatenate([columns, columns], axis=0))
    spec = second_stage(
        [stage[:, cols * c : cols * (c + 1)] for c in range(8)],
        twid_cos, twid_sin, second_ref[...],
    )

    def parts_of(array, c):
        block = array[rows * c : rows * (c + 1)]
        return block[:, :cols], block[:, cols:]

    def inverse_of(products):
        pieces = []
        for real, imag in products:
            value = jnp.concatenate([real, imag], axis=1).astype(BF)
            pieces.append(jnp.concatenate([value, value], axis=1))
        turned = dot32(jnp.concatenate(pieces, axis=0), inverse_ref[...])
        columns = []
        for c in range(len(products)):
            real, imag = parts_of(turned, c)
            value = jnp.concatenate(
                [real * twid_cos - imag * twid_sin, imag * twid_cos + real * twid_sin], axis=0
            ).astype(BF)
            columns.append(jnp.concatenate([value, value], axis=0))
        return dot32(last_ref[...], jnp.concatenate(columns, axis=1))

    convs, backs, corrs = [], [], []
    for c in range(4):
        tap_r, tap_i = parts_of(spec_ref, c)
        in_r, in_i = parts_of(spec, c)
        gr_r, gr_i = parts_of(spec, 4 + c)
        convs.append((tap_r * in_r - tap_i * in_i, tap_r * in_i + tap_i * in_r))
        backs.append((tap_r * gr_r + tap_i * gr_i, tap_r * gr_i - tap_i * gr_r))
        corrs.append((in_r * gr_r + in_i * gr_i, in_r * gr_i - in_i * gr_r))
    result = inverse_of(convs + backs)
    for c in range(8):
        back_ref[pl.ds(c, rows, stride=8), :] = result[:, cols * c : cols * (c + 1)]
    done_ref[...] = back_ref[...].astype(BF)
    copy = pltpu.make_async_copy(done_ref, send_ref, sem)
    copy.start()
    result = inverse_of(corrs)
    for c in range(4):
        corr_mix_ref[pl.ds(c, rows, stride=4), :] = result[:, cols * c : cols * (c + 1)]
    corr_ref[...] = corr_mix_ref[...].astype(BF)
    copy.wait()


def gate_kernel(
    flip, recv_ref, outer_ref, inner_ref, signal_ref, cotan_ref, part_ref,
    mixed_ref, gouter_ref, ginner_ref, gsignal_ref, gfilter_ref, flat_ref, mix_ref,
):
    total = part_ref[0].astype(F32)
    for g in range(1, part_ref.shape[0]):
        total = total + part_ref[g].astype(F32)
    count = recv_ref.shape[0] // 8
    cols = recv_ref.shape[1]
    for n in range(count):
        gfilter_ref[:, cols * (n ^ flip) : cols * ((n ^ flip) + 1)] = total[4 * n : 4 * n + 4, :]

    def store(rows, value):
        flat_ref[rows, :] = value

    flipped_copy(store, lambda rows: recv_ref[rows, :].astype(F32), count, flip, 8)
    for c in range(8):
        mix_ref[c // 4, pl.ds(c % 4, count, stride=4), :] = flat_ref[pl.ds(c, count, stride=8), :]
    conv = mix_ref[0].T
    prod = mix_ref[1].T
    mixed_ref[...] = (outer_ref[...].astype(F32) * conv).astype(BF)
    gouter_ref[...] = (cotan_ref[...].astype(F32) * conv).astype(BF)
    ginner_ref[...] = (prod * signal_ref[...].astype(F32)).astype(BF)
    gsignal_ref[...] = (prod * inner_ref[...].astype(F32)).astype(BF)


def call(kernel, out_shape, scratch, flops=0, nbytes=0, vmem=VMEM_BYTES, **specs):
    return pl.pallas_call(
        kernel,
        out_shape=out_shape,
        scratch_shapes=scratch,
        compiler_params=pltpu.CompilerParams(vmem_limit_bytes=vmem),
        **specs,
        cost_estimate=pl.CostEstimate(flops=flops, bytes_accessed=nbytes, transcendentals=0),
    )


def exchange(chunks, order):
    return lax.all_to_all(chunks, "seq", 0, 0, axis_index_groups=[order], tiled=True)


def body(gate_outer, gate_inner, signal, filter_raw, cotangent):
    tok_rows, chan_cols = gate_outer.shape
    seq_parts = lax.axis_size("seq")
    rows, cols = seq_parts, tok_rows
    seq_len = rows * cols
    order, flip = member_order(seq_parts)
    tables = dft_tables(rows, cols, 1.0 / math.sqrt(seq_len) / seq_len, order)
    first, twid = jnp.asarray(tables["first"]), jnp.asarray(tables["twid"])
    second, inverse = jnp.asarray(tables["second"]), jnp.asarray(tables["inverse"])
    last = jnp.asarray(tables["last"])
    wide = 8 * rows
    packed = call(
        functools.partial(pack_kernel, flip),
        jax.ShapeDtypeStruct((wide, cols), BF),
        [
            pltpu.VMEM((4, tok_rows, chan_cols), BF),
            pltpu.VMEM((2, chan_cols, tok_rows), F32),
            pltpu.VMEM((wide, cols), F32),
            pltpu.SemaphoreType.DMA((4,)),
        ],
        nbytes=6 * 2 * tok_rows * chan_cols,
        vmem=VMEM_MOST,
        in_specs=[pl.BlockSpec(memory_space=pltpu.HBM)] * 4,
    )(gate_outer, gate_inner, signal, cotangent)
    received = exchange(packed.reshape(rows, 8, cols), order)
    tap_spec = call(
        functools.partial(filter_kernel, flip),
        jax.ShapeDtypeStruct((4 * rows, 2 * cols), F32),
        [pltpu.VMEM((4 * rows, cols), F32)],
        flops=10**9, nbytes=10**6,
    )(filter_raw, first, twid, second)
    send, corr = call(
        conv_kernel,
        (
            jax.ShapeDtypeStruct((wide, cols), BF),
            jax.ShapeDtypeStruct((4 * rows, cols), BF),
        ),
        [
            pltpu.VMEM((wide, cols), F32),
            pltpu.VMEM((wide, cols), F32),
            pltpu.VMEM((4 * rows, cols), F32),
            pltpu.VMEM((wide, cols), BF),
            pltpu.SemaphoreType.DMA,
        ],
        flops=3 * 10**9, nbytes=2 * 10**6,
        out_specs=(
            pl.BlockSpec(memory_space=pltpu.HBM),
            pl.BlockSpec(memory_space=pltpu.VMEM),
        ),
    )(received.reshape(wide, cols), tap_spec, first, twid, second, inverse, last)
    parts = lax.all_gather(corr, "chan", axis=0, tiled=False)
    returned = exchange(send.reshape(rows, 8, cols), order)
    block = jax.ShapeDtypeStruct((tok_rows, chan_cols), BF)
    return call(
        functools.partial(gate_kernel, flip),
        (block, block, block, block, jax.ShapeDtypeStruct(filter_raw.shape, F32)),
        [pltpu.VMEM((wide, cols), F32), pltpu.VMEM((2, chan_cols, tok_rows), F32)],
        nbytes=12 * 2 * tok_rows * chan_cols,
    )(returned.reshape(wide, cols), gate_outer, gate_inner, signal, cotangent, parts)


def solution(mesh):
    in_specs = (
        P("seq", "chan"),
        P("seq", "chan"),
        P("seq", "chan"),
        P("seq", None),
        P("seq", "chan"),
    )
    out_specs = (
        P("seq", "chan"),
        P("seq", "chan"),
        P("seq", "chan"),
        P("seq", "chan"),
        P("seq", None),
    )
    return jax.shard_map(body, mesh=mesh, in_specs=in_specs, out_specs=out_specs, check_vma=False)
```

```python
import functools
import math

import jax
import jax.numpy as jnp
import numpy as np
import ml_dtypes
from jax import lax
from jax.experimental import pallas as pl
from jax.experimental.pallas import tpu as pltpu
from jax.sharding import PartitionSpec as P

BF = jnp.bfloat16
F32 = jnp.float32
VMEM_BYTES = 40 * 1024 * 1024
VMEM_MOST = 60 * 1024 * 1024


def member_order(count):
    flip = count // 2 + count // 8
    return [r ^ flip for r in range(count)], flip


def flipped_copy(store, load, count, flip, height):
    run = flip & -flip if flip else count
    for start in range(0, count, run):
        source = start ^ flip
        store(slice(start * height, (start + run) * height), load(slice(source * height, (source + run) * height)))


def split_np(table):
    high = table.astype(ml_dtypes.bfloat16)
    low = (table - high.astype(np.float64)).astype(ml_dtypes.bfloat16)
    return high, low


def dft_tables(rows_n, cols_n, scale, order):
    length = rows_n * cols_n
    row_i = np.arange(rows_n, dtype=np.float64)
    col_i = np.arange(cols_n, dtype=np.float64)
    ang_one = -2.0 * np.pi * np.outer(row_i + 0.25, row_i[order]) / rows_n
    ang_twid = -2.0 * np.pi * np.outer(row_i + 0.25, col_i) / length
    ang_two = 2.0 * np.pi * (np.outer(col_i, col_i) % cols_n) / cols_n
    first = np.concatenate([np.cos(ang_one), np.sin(ang_one)], axis=0)
    cos_two, sin_two = np.cos(ang_two), np.sin(ang_two)
    second = np.block([[cos_two, -sin_two], [sin_two, cos_two]])
    second_inv = second.T
    last = first.T * scale
    first_h, first_l = split_np(first)
    second_h, second_l = split_np(second)
    inv_h, inv_l = split_np(second_inv)
    last_h, last_l = split_np(last)
    return dict(
        first=np.concatenate([first_h, first_l], axis=1),
        twid=np.concatenate([np.cos(ang_twid), -np.sin(ang_twid)], axis=1).astype(np.float32),
        second=np.concatenate([second_h, second_h, second_l], axis=0),
        inverse=np.concatenate([inv_h, inv_l], axis=0),
        last=np.concatenate([last_h, last_l], axis=1),
    )


def split_hl(value):
    high = value.astype(BF)
    low = (value - high.astype(F32)).astype(BF)
    return high, low


def dot32(left, right):
    return lax.dot_general(left, right, (((1,), (0,)), ((), ())), preferred_element_type=F32)


def pack_kernel(
    flip, outer_ref, inner_ref, signal_ref, cotan_ref, out_ref, held_ref, flat_ref, mix_ref, sems
):
    count = out_ref.shape[0] // 8
    sources = (inner_ref, signal_ref, cotan_ref, outer_ref)
    copies = [
        pltpu.make_async_copy(ref, held_ref.at[k], sems.at[k]) for k, ref in enumerate(sources)
    ]
    for copy in copies:
        copy.start()
    for half in range(2):
        copies[2 * half].wait()
        copies[2 * half + 1].wait()
        left, right = held_ref[2 * half].astype(F32), held_ref[2 * half + 1].astype(F32)
        flat_ref[half] = (left * right).astype(BF).astype(F32).T
        for c in range(4):
            mix_ref[pl.ds(4 * half + c, count, stride=8), :] = flat_ref[
                half, pl.ds(c, count, stride=4), :
            ]

    def store(rows, value):
        out_ref[rows, :] = value

    flipped_copy(store, lambda rows: mix_ref[rows, :].astype(BF), count, flip, 8)


def second_stage(part, twid_cos, twid_sin, second):
    rows = twid_cos.shape[0]
    pieces = []
    for one in part:
        real, imag = one[:rows], one[rows:]
        turned = jnp.concatenate(
            [real * twid_cos + imag * twid_sin, imag * twid_cos - real * twid_sin], axis=1
        )
        high, low = split_hl(turned)
        pieces.append(jnp.concatenate([high, low, high], axis=1))
    return dot32(jnp.concatenate(pieces, axis=0), second)


def filter_kernel(flip, filt_ref, first_ref, twid_ref, second_ref, out_ref, rows_ref):
    rows = twid_ref.shape[0]
    cols = twid_ref.shape[1] // 2
    for n in range(rows):
        rows_ref[pl.ds(4 * (n ^ flip), 4), :] = filt_ref[:, cols * n : cols * (n + 1)]
    first = first_ref[...]
    parts = []
    for f in range(4):
        high, low = split_hl(rows_ref[pl.ds(f, rows, stride=4), :])
        parts.append((high, low))
    high = jnp.concatenate([h for h, _ in parts], axis=1)
    low = jnp.concatenate([l for _, l in parts], axis=1)
    stage = dot32(first, jnp.concatenate([high, high], axis=0)) + dot32(first[:, :rows], low)
    out_ref[...] = second_stage(
        [stage[:, cols * f : cols * (f + 1)] for f in range(4)],
        twid_ref[:, :cols],
        twid_ref[:, cols:],
        second_ref[...],
    )


def conv_kernel(
    recv_ref, spec_ref, first_ref, twid_ref, second_ref, inverse_ref, last_ref,
    send_ref, corr_ref, flat_ref, back_ref, corr_mix_ref, done_ref, sem,
):
    rows = twid_ref.shape[0]
    cols = twid_ref.shape[1] // 2
    twid_cos, twid_sin = twid_ref[:, :cols], twid_ref[:, cols:]
    flat_ref[...] = recv_ref[...].astype(F32)
    columns = jnp.concatenate(
        [flat_ref[pl.ds(c, rows, stride=8), :].astype(BF) for c in range(8)], axis=1
    )
    stage = dot32(first_ref[...], jnp.concatenate([columns, columns], axis=0))
    spec = second_stage(
        [stage[:, cols * c : cols * (c + 1)] for c in range(8)],
        twid_cos, twid_sin, second_ref[...],
    )

    def parts_of(array, c):
        block = array[rows * c : rows * (c + 1)]
        return block[:, :cols], block[:, cols:]

    def inverse_of(products):
        pieces = []
        for real, imag in products:
            value = jnp.concatenate([real, imag], axis=1).astype(BF)
            pieces.append(jnp.concatenate([value, value], axis=1))
        turned = dot32(jnp.concatenate(pieces, axis=0), inverse_ref[...])
        columns = []
        for c in range(len(products)):
            real, imag = parts_of(turned, c)
            value = jnp.concatenate(
                [real * twid_cos - imag * twid_sin, imag * twid_cos + real * twid_sin], axis=0
            ).astype(BF)
            columns.append(jnp.concatenate([value, value], axis=0))
        return dot32(last_ref[...], jnp.concatenate(columns, axis=1))

    convs, backs, corrs = [], [], []
    for c in range(4):
        tap_r, tap_i = parts_of(spec_ref, c)
        in_r, in_i = parts_of(spec, c)
        gr_r, gr_i = parts_of(spec, 4 + c)
        convs.append((tap_r * in_r - tap_i * in_i, tap_r * in_i + tap_i * in_r))
        backs.append((tap_r * gr_r + tap_i * gr_i, tap_r * gr_i - tap_i * gr_r))
        corrs.append((in_r * gr_r + in_i * gr_i, in_r * gr_i - in_i * gr_r))
    result = inverse_of(convs + backs)
    for c in range(8):
        back_ref[pl.ds(c, rows, stride=8), :] = result[:, cols * c : cols * (c + 1)]
    done_ref[...] = back_ref[...].astype(BF)
    copy = pltpu.make_async_copy(done_ref, send_ref, sem)
    copy.start()
    result = inverse_of(corrs)
    for c in range(4):
        corr_mix_ref[pl.ds(c, rows, stride=4), :] = result[:, cols * c : cols * (c + 1)]
    corr_ref[...] = corr_mix_ref[...].astype(BF)
    copy.wait()


def gate_kernel(
    flip, recv_ref, outer_ref, inner_ref, signal_ref, cotan_ref, part_ref,
    mixed_ref, gouter_ref, ginner_ref, gsignal_ref, gfilter_ref, flat_ref, mix_ref,
):
    total = part_ref[0].astype(F32)
    for g in range(1, part_ref.shape[0]):
        total = total + part_ref[g].astype(F32)
    count = recv_ref.shape[0] // 8
    cols = recv_ref.shape[1]
    for n in range(count):
        gfilter_ref[:, cols * (n ^ flip) : cols * ((n ^ flip) + 1)] = total[4 * n : 4 * n + 4, :]

    def store(rows, value):
        flat_ref[rows, :] = value

    flipped_copy(store, lambda rows: recv_ref[rows, :].astype(F32), count, flip, 8)
    for c in range(8):
        mix_ref[c // 4, pl.ds(c % 4, count, stride=4), :] = flat_ref[pl.ds(c, count, stride=8), :]
    conv = mix_ref[0].T
    prod = mix_ref[1].T
    mixed_ref[...] = (outer_ref[...].astype(F32) * conv).astype(BF)
    gouter_ref[...] = (cotan_ref[...].astype(F32) * conv).astype(BF)
    ginner_ref[...] = (prod * signal_ref[...].astype(F32)).astype(BF)
    gsignal_ref[...] = (prod * inner_ref[...].astype(F32)).astype(BF)


def call(kernel, out_shape, scratch, flops=0, nbytes=0, vmem=VMEM_BYTES, **specs):
    return pl.pallas_call(
        kernel,
        out_shape=out_shape,
        scratch_shapes=scratch,
        compiler_params=pltpu.CompilerParams(vmem_limit_bytes=vmem),
        **specs,
        cost_estimate=pl.CostEstimate(flops=flops, bytes_accessed=nbytes, transcendentals=0),
    )


def exchange(chunks, order):
    return lax.all_to_all(chunks, "seq", 0, 0, axis_index_groups=[order], tiled=True)


def body(gate_outer, gate_inner, signal, filter_raw, cotangent):
    tok_rows, chan_cols = gate_outer.shape
    seq_parts = lax.axis_size("seq")
    rows, cols = seq_parts, tok_rows
    seq_len = rows * cols
    order, flip = member_order(seq_parts)
    tables = dft_tables(rows, cols, 1.0 / math.sqrt(seq_len) / seq_len, order)
    first, twid = jnp.asarray(tables["first"]), jnp.asarray(tables["twid"])
    second, inverse = jnp.asarray(tables["second"]), jnp.asarray(tables["inverse"])
    last = jnp.asarray(tables["last"])
    wide = 8 * rows
    packed = call(
        functools.partial(pack_kernel, flip),
        jax.ShapeDtypeStruct((wide, cols), BF),
        [
            pltpu.VMEM((4, tok_rows, chan_cols), BF),
            pltpu.VMEM((2, chan_cols, tok_rows), F32),
            pltpu.VMEM((wide, cols), F32),
            pltpu.SemaphoreType.DMA((4,)),
        ],
        nbytes=6 * 2 * tok_rows * chan_cols,
        vmem=VMEM_MOST,
        in_specs=[pl.BlockSpec(memory_space=pltpu.HBM)] * 4,
    )(gate_outer, gate_inner, signal, cotangent)
    received = exchange(packed.reshape(rows, 8, cols), order)
    tap_spec = call(
        functools.partial(filter_kernel, flip),
        jax.ShapeDtypeStruct((4 * rows, 2 * cols), F32),
        [pltpu.VMEM((4 * rows, cols), F32)],
        flops=10**9, nbytes=10**6,
    )(filter_raw, first, twid, second)
    send, corr = call(
        conv_kernel,
        (
            jax.ShapeDtypeStruct((wide, cols), BF),
            jax.ShapeDtypeStruct((4 * rows, cols), BF),
        ),
        [
            pltpu.VMEM((wide, cols), F32),
            pltpu.VMEM((wide, cols), F32),
            pltpu.VMEM((4 * rows, cols), F32),
            pltpu.VMEM((wide, cols), BF),
            pltpu.SemaphoreType.DMA,
        ],
        flops=3 * 10**9, nbytes=2 * 10**6,
        out_specs=(
            pl.BlockSpec(memory_space=pltpu.HBM),
            pl.BlockSpec(memory_space=pltpu.VMEM),
        ),
    )(received.reshape(wide, cols), tap_spec, first, twid, second, inverse, last)
    parts = lax.all_gather(corr, "chan", axis=0, tiled=False)
    returned = exchange(send.reshape(rows, 8, cols), order)
    block = jax.ShapeDtypeStruct((tok_rows, chan_cols), BF)
    return call(
        functools.partial(gate_kernel, flip),
        (block, block, block, block, jax.ShapeDtypeStruct(filter_raw.shape, F32)),
        [pltpu.VMEM((wide, cols), F32), pltpu.VMEM((2, chan_cols, tok_rows), F32)],
        nbytes=12 * 2 * tok_rows * chan_cols,
    )(returned.reshape(wide, cols), gate_outer, gate_inner, signal, cotangent, parts)


def solution(mesh):
    in_specs = (
        P("seq", "chan"),
        P("seq", "chan"),
        P("seq", "chan"),
        P("seq", None),
        P("seq", "chan"),
    )
    out_specs = (
        P("seq", "chan"),
        P("seq", "chan"),
        P("seq", "chan"),
        P("seq", "chan"),
        P("seq", None),
    )
    return jax.shard_map(body, mesh=mesh, in_specs=in_specs, out_specs=out_specs, check_vma=False)
```
